32 devices in a mesh: grp: 2 (over y), sec: 4 (over z), col: 2 (over x), rep: 2 (over core).
Axes of the slice: x: 2, y: 2, z: 4, core: 2. Of those that a mesh axis runs over, the one named last changes fastest.
Arguments:
- corners: bfloat16 [4, 2, 4, 128, 128], P(('grp', 'col'), None, 'sec', 'rep'), parts along dimension 0, may hold values from -6 to 6
- edges: bfloat16 [4, 2, 4, 128, 6272], P(('grp', 'col'), None, 'sec'), parts along dimension 0, may hold values from -0.5 to 0.5
- projectors: bfloat16 [4, 2, 4, 128, 6272], P(('grp', 'col'), None, 'sec', 'rep'), parts along dimension 0, may hold values from -0.078125 to 0.078125
- sector_sizes: int32 [4], replicated, may hold values from 1 to 128, 192 in all
Outputs:
- new_corners: bfloat16 [4, 2, 4, 128, 128], P(('grp', 'col'), None, 'sec', 'rep'), parts along dimension 0
- log_scales: float32 [4, 2, 4], P(('grp', 'col')), parts along dimension 0
The draws below stay inside these ranges and needn't reach their ends.
There are 2 independent parts, one for each index of `grp`. The reference program is written for one: setup_inputs(seed, part) draws one part's arguments, and reference() takes and returns one part's arrays. A program takes and returns all parts, laid end to end along the dimension named above; an argument that names none is the same for every part. Nothing has to cross between parts.
Inputs may be any that keep to these rules, and one draw needn't show every extreme that they name: `sector_sizes`: sector sizes sum to 192; the largest is exactly 128.
All inputs are finite; a program needn't handle non-finite values.
Results may differ from the reference program's by a relative error of at most 0.013.
Values may be sent and summed in bfloat16 or wider, within the bound.
A program may use at most 64 MiB of HBM per device.

```python
import math
import jax
import jax.numpy as jnp
import numpy as np
from jax import lax

BLOCK = 128
K_NEG = 16
K_ZERO = 17
ITERS = 4
D2 = 49
SECTORS = 4
CHI = 192
NCOL = 2


def level_of(key, shape, shards, smallest, largest):
    level, own = 1.0, jax.random.fold_in(key, 6)
    for dim, blocks in shards:
        heights = jnp.exp(jax.random.uniform(jax.random.fold_in(own, dim), (blocks,), jnp.float32, smallest / len(shards), largest / len(shards)))
        level = level * jnp.repeat(heights, shape[dim] // blocks).reshape([-1 if axis == dim else 1 for axis in range(len(shape))])
    return level


def split_up(count, total, limit, skew):
    portions = [(1 << 20) // math.isqrt(grade ** skew) + 1 for grade in range(2, count + 1)]
    surplus, counts = total - limit - (count - 1), [1] * (count - 1)
    while surplus > 0:
        candidates = [i for i in range(count - 1) if counts[i] < limit]
        whole, left = sum([portions[i] for i in candidates]), surplus
        for i in candidates:
            extra = min(limit - counts[i], max(1, left * portions[i] // whole), surplus)
            counts[i] = counts[i] + extra
            surplus = surplus - extra
    return np.array([limit] + counts)


def ragged_sizes(key, number_of, total, most, skew):
    if number_of == 2:
        one = jax.random.randint(key, (), max(1, total - most), min(most, total - 1) + 1)
        return jnp.stack([one, total - one])
    tallies = jnp.asarray(split_up(number_of, total, most, skew), jnp.int32)
    pairs = (number_of - 1) // 2
    giver, receiver = tallies[1:1 + 2 * pairs:2], tallies[2:2 + 2 * pairs:2]
    slack = jnp.minimum(giver - 1, most - receiver)
    passed = jax.random.randint(jax.random.fold_in(key, 1), (pairs,), 0, 1 << 20) % (slack + 1)
    tallies = tallies.at[1:1 + 2 * pairs:2].set(giver - passed).at[2:2 + 2 * pairs:2].set(receiver + passed)
    return tallies[jax.random.permutation(jax.random.fold_in(key, 2), number_of)]


def noise(own_key, dims, deviation, limit, split=(), dtype=jnp.bfloat16):
    drawn = jax.random.normal(own_key, dims, jnp.float32) * deviation
    if len(split) > 0:
        drawn = level_of(own_key, dims, split, -0.22, 0.18) * drawn
    return jnp.clip(drawn, min=-limit, max=limit).astype(dtype)


def setup_inputs(seed: int = 0, part: int = 0) -> dict:
    arg_keys = jax.random.split(jax.random.key(seed), 5)
    own_keys = jax.random.split(jax.random.fold_in(arg_keys[4], part), 5)
    return {
        "corners": noise(own_keys[0], (NCOL, 2, SECTORS, BLOCK, BLOCK), 1.0, 6.0, ((0, 2), (2, 4), (3, 2))),
        "edges": noise(own_keys[1], (NCOL, 2, SECTORS, BLOCK, D2 * BLOCK), BLOCK ** -0.5, 0.5, ((0, 2), (2, 4))),
        "projectors": noise(own_keys[2], (NCOL, 2, SECTORS, BLOCK, D2 * BLOCK), (D2 * BLOCK) ** -0.5, 0.078125, ((0, 2), (2, 4), (3, 2))),
        "sector_sizes": ragged_sizes(arg_keys[3], SECTORS, CHI, BLOCK, 2).astype(jnp.int32),
    }


def contract(proj_part, block_part):
    return jnp.einsum('rsakp,rsakb->rspb', proj_part.astype(jnp.float32), block_part.astype(jnp.float32))

def move_column(corner, edge, projector, keep, count):
    absorbed = jnp.einsum('rsax,rsxn->rsan', corner.astype(jnp.float32), edge.astype(jnp.float32)).astype(jnp.bfloat16)
    shaped = absorbed.reshape(2, SECTORS, BLOCK, D2, BLOCK)
    proj = projector.reshape(2, SECTORS, BLOCK, D2, BLOCK)
    rise = K_NEG + K_ZERO
    zero = jnp.zeros_like(shaped[:, :1])
    from_lower = jnp.concatenate([zero, shaped[:, :-1]], axis=1)[:, :, :, rise:, :]
    from_upper = jnp.concatenate([shaped[:, 1:], zero], axis=1)[:, :, :, :K_NEG, :]
    own_part = shaped[:, :, :, K_NEG:rise, :]
    summed = contract(proj[:, :, :, rise:, :], from_lower)
    summed = summed + contract(proj[:, :, :, K_NEG:rise, :], own_part)
    summed = summed + contract(proj[:, :, :, :K_NEG, :], from_upper)
    masked = jnp.where(keep[None], summed, jnp.float32(0.0))
    scale = lax.optimization_barrier(jnp.sum(masked * masked, axis=(1, 2, 3)))
    factor = scale / count + 1e-06
    fresh = masked / jnp.sqrt(factor)[:, None, None, None]
    return (fresh.astype(jnp.bfloat16), jnp.log(factor))

def reference(corners, edges, projectors, sector_sizes):
    slots = jnp.arange(BLOCK)
    keep = (slots[None, :, None] < sector_sizes[:, None, None]) & (slots[None, None, :] < sector_sizes[:, None, None])
    count = jnp.sum(sector_sizes.astype(jnp.float32) ** 2)
    current = jnp.where(keep[None, None], corners, jnp.zeros_like(corners)).astype(jnp.bfloat16)
    logs = []
    for step in range(ITERS):
        fresh, log_now = lax.map(lambda trio: move_column(trio[0], trio[1], trio[2], keep, count), (current, edges, projectors))
        logs.append(log_now)
        current = jnp.roll(fresh, 1, axis=0)
    return (current, jnp.stack(logs, axis=-1))
```

```python
import functools

import jax
import jax.numpy as jnp
from jax import lax
from jax.experimental import pallas as pl
from jax.experimental.pallas import tpu as pltpu
from jax.sharding import PartitionSpec as P

K_NEG = 16
K_ZERO = 17
ITERS = 4
MESH = pl.DeviceIdType.MESH
F32 = jnp.float32
BF16 = jnp.bfloat16


def rolled(x, axis):
    half = x.shape[axis] // 2
    lo = lax.slice_in_dim(x, 0, half, axis=axis)
    hi = lax.slice_in_dim(x, half, 2 * half, axis=axis)
    return jnp.concatenate([hi, lo], axis=axis)


def kernel(
    ncol, nsec, block, states, narrow,
    sizes, corners, edges, projectors,
    out, logs,
    own, stage, packed, halo, proj, projt, first, cur, sent, scale, tiles, fin, last, all_last, last_tile,
    load_sem, halo_send, halo_recv, proj_send, proj_recv, first_send, first_recv,
    cur_send, cur_recv, scale_send, scale_recv, fin_send, fin_recv, next_send, next_recv, log_send, log_recv,
):
    half = block // 2
    rise = K_NEG + K_ZERO
    wide = K_NEG * block // 2
    c, t, r = lax.axis_index("col"), lax.axis_index("sec"), lax.axis_index("rep")
    other = 1 - r
    right = lax.rem(c + 1, ncol)
    pair = 2 * nsec
    me = t * 2 + r

    load_own = pltpu.make_async_copy(
        edges.at[r, :, K_NEG * block : rise * block], own, load_sem.at[0]
    )
    load_proj = pltpu.make_async_copy(projectors.at[r], proj.at[r], load_sem.at[1])
    loads = []
    if narrow:
        loads = [
            pltpu.make_async_copy(edges.at[r, :, rise * block :], stage.at[0], load_sem.at[2]),
            pltpu.make_async_copy(edges.at[r, :, : K_NEG * block], stage.at[1], load_sem.at[3]),
        ]
    for copy in loads + [load_proj, load_own]:
        copy.start()

    barrier = pltpu.get_barrier_semaphore()
    everyone = ncol * pair
    spot = c * pair + me

    @pl.loop(1, everyone)
    def _(step):
        to = lax.rem(spot + step, everyone)
        pl.semaphore_signal(
            barrier, inc=1,
            device_id={"col": to // pair, "sec": lax.rem(to, pair) // 2, "rep": lax.rem(to, 2)},
            device_id_type=MESH,
        )

    live = sizes[t]
    count = jnp.float32(0.0)
    for s in range(nsec):
        size = sizes[s].astype(F32)
        count = count + size * size
    rows = lax.broadcasted_iota(jnp.int32, (block, block), 0)
    lanes = lax.broadcasted_iota(jnp.int32, (block, block), 1)
    keep = (rows < live) & (lanes < live)
    half_rows = lax.broadcasted_iota(jnp.int32, (half, block), 0) + r * half
    half_lanes = lax.broadcasted_iota(jnp.int32, (half, block), 1)
    half_keep = (half_rows < live) & (half_lanes < live)
    for which in range(2):
        value = corners[which].astype(F32)
        first[which] = jnp.where(half_keep, value, 0.0).astype(BF16)

    @pl.when(t == 0)
    def _():
        cur[:, 0] = jnp.zeros((ITERS, 2, half, block), BF16)
        halo[0] = jnp.zeros((2, block, wide), BF16)

    @pl.when(t == nsec - 1)
    def _():
        cur[:, 2] = jnp.zeros((ITERS, 2, half, block), BF16)
        halo[1] = jnp.zeros((2, block, wide), BF16)

    pl.semaphore_wait(barrier, everyone - 1)

    has_low, has_high = t > 0, t < nsec - 1

    def guarded(dt, action):
        if dt == 0:
            action()
        else:
            pl.when(has_high if dt > 0 else has_low)(action)

    send_proj = pltpu.make_async_remote_copy(
        src_ref=projectors.at[other], dst_ref=proj.at[r],
        send_sem=proj_send, recv_sem=proj_recv,
        device_id={"rep": other}, device_id_type=MESH,
    )
    send_proj.start()

    def first_copy(dt, which):
        side = r if which == 0 else other
        return pltpu.make_async_remote_copy(
            src_ref=first.at[side], dst_ref=cur.at[0, 1 - dt, r],
            send_sem=first_send.at[dt + 1, which], recv_sem=first_recv.at[1 - dt, which],
            device_id={"sec": t + dt, "rep": side}, device_id_type=MESH,
        )

    firsts = [(0, 1), (1, 0), (1, 1), (-1, 0), (-1, 1)]
    for dt, which in firsts:
        guarded(dt, lambda dt=dt, which=which: first_copy(dt, which).start())
    cur[0, 1, r] = first[r]

    def halo_copy(side, part):
        if narrow:
            src = packed.at[side]
        else:
            start = (rise * block if side == 0 else 0) + part * wide
            src = edges.at[r, :, start : start + wide]
        return pltpu.make_async_remote_copy(
            src_ref=src, dst_ref=halo.at[side, part],
            send_sem=halo_send.at[side, part], recv_sem=halo_recv.at[side, part],
            device_id={"sec": t + 1 - 2 * side}, device_id_type=MESH,
        )

    parts = 1 if narrow else 2
    for side in range(2):
        if narrow:
            loads[side].wait()
            for j in range(K_NEG // 2):
                low = stage[side, :, j * block : (j + 1) * block]
                high = stage[side, :, wide + j * block : wide + (j + 1) * block]
                by_row = jnp.concatenate([low[:half], high[:half]], axis=0)
                by_lane = jnp.concatenate([low[:, :half], high[:, :half]], axis=1)
                mixed = jnp.where(live > half, by_lane.astype(F32), by_row.astype(F32))
                packed[side, :, j * block : (j + 1) * block] = mixed.astype(BF16)

        def go(side=side):
            for part in range(parts):
                halo_copy(side, part).start()

        guarded(1 - 2 * side, go)

    load_proj.wait()
    send_proj.wait_recv()
    for k in range(states):
        piece = proj[:, :, k * block : (k + 1) * block].reshape(block, block)
        projt[:, k * block : (k + 1) * block] = piece.T
    load_own.wait()

    def part_of(corner, edge, start):
        number = edge.shape[1] // block
        absorbed = jnp.dot(corner, edge, preferred_element_type=F32).astype(BF16)
        stacked = jnp.concatenate(
            [absorbed[:, k * block : (k + 1) * block] for k in range(number)], axis=0
        )
        left = projt[:, start * block : (start + number) * block]
        return jnp.dot(left, stacked, preferred_element_type=F32)

    def halo_ready(side):
        def wait():
            for part in range(parts):
                halo_copy(side, part).wait_recv()

        guarded(2 * side - 1, wait)
        if narrow:
            source = jnp.clip(t - 1 + 2 * side, 0, nsec - 1)
            wide_rows = sizes[source] > half

            for j in range(K_NEG // 2):
                piece = halo[side, 0, :, j * block : (j + 1) * block]
                by_row, by_lane = rolled(piece, 0), rolled(piece, 1)
                mixed = jnp.where(wide_rows, by_lane.astype(F32), by_row.astype(F32))
                halo[side, 1, :, j * block : (j + 1) * block] = mixed.astype(BF16)

    def cur_copy(move, dt):
        return pltpu.make_async_remote_copy(
            src_ref=sent.at[move], dst_ref=cur.at[move + 1, 1 - dt],
            send_sem=cur_send.at[move, dt + 1], recv_sem=cur_recv.at[move, 1 - dt],
            device_id={"col": right, "sec": t + dt}, device_id_type=MESH,
        )

    def scale_copy(move, step):
        to = lax.rem(t + step, nsec)
        return pltpu.make_async_remote_copy(
            src_ref=tiles.at[move], dst_ref=scale.at[move, t],
            send_sem=scale_send.at[move, step], recv_sem=scale_recv.at[move, t],
            device_id={"col": right, "sec": to}, device_id_type=MESH,
        )

    def fin_copy(piece):
        return pltpu.make_async_remote_copy(
            src_ref=sent.at[ITERS - 1, piece], dst_ref=fin.at[r],
            send_sem=fin_send.at[piece], recv_sem=fin_recv.at[r],
            device_id={"col": right, "rep": jnp.int32(piece)}, device_id_type=MESH,
        )

    def spread_copy(step, same):
        to = lax.rem(me + step, pair)
        where = {"sec": to // 2, "rep": lax.rem(to, 2)}
        if not same:
            where["col"] = right
        sems, got, dst = (log_send, log_recv, all_last) if same else (next_send, next_recv, last)
        return pltpu.make_async_remote_copy(
            src_ref=last_tile, dst_ref=dst.at[me],
            send_sem=sems.at[step], recv_sem=got.at[me],
            device_id=where, device_id_type=MESH,
        )

    def arrived(ref, sem):
        pltpu.make_async_copy(ref, ref, sem).wait()

    def corner_ready(move, j):
        def wait():
            if move == 0:
                for which in range(2):
                    if j == 1 and which == 0:
                        continue
                    spot_ = cur.at[0, j, r if which == 0 else other]
                    arrived(spot_, first_recv.at[j, which])
            else:
                arrived(cur.at[move, j], cur_recv.at[move - 1, j])

        guarded(j - 1, wait)
        return cur[move, j].reshape(block, block)

    sums = []
    for move in range(ITERS):
        total = part_of(corner_ready(move, 1), own[...], K_NEG)
        for side, j, start in ((0, 0, rise), (1, 2, 0)):
            corner = corner_ready(move, j)
            if move == 0:
                halo_ready(side)
            for part in range(2):
                total = total + part_of(corner, halo[side, part], start + part * K_NEG // 2)
        if move > 0:
            for s in range(nsec):
                arrived(scale.at[move - 1, s], scale_recv.at[move - 1, s])
            whole = jnp.sum(jnp.sum(scale[move - 1], axis=0), keepdims=True)
            total = total / jnp.sqrt(whole / count + 1e-06)
        masked = jnp.where(keep, total, 0.0)
        sent[move] = masked.astype(BF16).reshape(2, half, block)
        if move < ITERS - 1:
            for dt in (1, -1, 0):
                guarded(dt, lambda dt=dt, move=move: cur_copy(move, dt).start())
        else:
            for piece in range(2):
                fin_copy(piece).start()
        squares = jnp.sum((masked * masked).reshape(block // 8, 8, block), axis=0)
        sums.append(jnp.sum(squares, axis=0, keepdims=True))
        if move < ITERS - 1:
            tiles[move] = squares
            for step in range(nsec):
                scale_copy(move, step).start()

    last_tile[...] = jnp.concatenate(sums + [jnp.zeros((8 - ITERS, block), F32)], axis=0)
    for step in range(pair):
        spread_copy(step, False).start()
    for step in range(1, pair):
        spread_copy(step, True).start()
    all_last[me] = last_tile[...]

    for s in range(pair):
        arrived(last.at[s], next_recv.at[s])
    for side in range(2):
        arrived(fin.at[side], fin_recv.at[side])
        whole = last[side]
        for s in range(1, nsec):
            whole = whole + last[2 * s + side]
        whole = jnp.sum(whole[ITERS - 1 : ITERS, :], keepdims=True)
        out[side] = (fin[side].astype(F32) / jnp.sqrt(whole / count + 1e-06)).astype(BF16)

    for step in range(1, pair):
        source = lax.rem(me + step, pair)
        arrived(all_last.at[source], log_recv.at[source])
    diagonal = lax.broadcasted_iota(jnp.int32, (8, block), 0) == lax.broadcasted_iota(
        jnp.int32, (8, block), 1
    )
    for side in range(2):
        whole = all_last[side]
        for s in range(1, nsec):
            whole = whole + all_last[2 * s + side]
        value = jnp.log(jnp.sum(whole, axis=1, keepdims=True) / count + 1e-06)
        row = jnp.sum(jnp.where(diagonal, value, 0.0), axis=0, keepdims=True)
        logs[side : side + 1, :] = row[:, :ITERS]

    send_proj.wait_send()
    for dt, which in firsts:
        guarded(dt, lambda dt=dt, which=which: first_copy(dt, which).wait_send())
    for side in range(2):

        def gone(side=side):
            for part in range(parts):
                halo_copy(side, part).wait_send()

        guarded(1 - 2 * side, gone)
    for move in range(ITERS - 1):
        for dt in (1, -1, 0):
            guarded(dt, lambda dt=dt, move=move: cur_copy(move, dt).wait_send())
        for step in range(nsec):
            scale_copy(move, step).wait_send()
    for piece in range(2):
        fin_copy(piece).wait_send()
    for step in range(pair):
        spread_copy(step, False).wait_send()
    for step in range(1, pair):
        spread_copy(step, True).wait_send()


def on_device(ncol, nsec, corners, edges, projectors, sector_sizes):
    half, block = corners.shape[3:]
    width = edges.shape[4]
    states = width // block
    pair = 2 * nsec
    narrow = 48 * nsec - block - (nsec - 2) <= half
    wide = K_NEG * block // 2
    dma = pltpu.SemaphoreType.DMA
    vmem = pl.BlockSpec(memory_space=pltpu.VMEM)
    anywhere = pl.BlockSpec(memory_space=pl.ANY)
    parked = (2, block, 2 * wide) if narrow else (2, 16, block)
    packed = (2, block, wide) if narrow else (2, 16, block)
    new, logs = pl.pallas_call(
        functools.partial(kernel, ncol, nsec, block, states, narrow),
        out_shape=(
            jax.ShapeDtypeStruct((2, half, block), BF16),
            jax.ShapeDtypeStruct((2, ITERS), F32),
        ),
        in_specs=[pl.BlockSpec(memory_space=pltpu.SMEM), vmem, anywhere, anywhere],
        out_specs=(vmem, vmem),
        scratch_shapes=[
            pltpu.VMEM((block, K_ZERO * block), BF16),
            pltpu.VMEM(parked, BF16),
            pltpu.VMEM(packed, BF16),
            pltpu.VMEM((2, 2, block, wide), BF16),
            pltpu.VMEM((2, half, width), BF16),
            pltpu.VMEM((block, width), BF16),
            pltpu.VMEM((2, half, block), BF16),
            pltpu.VMEM((ITERS, 3, 2, half, block), BF16),
            pltpu.VMEM((ITERS, 2, half, block), BF16),
            pltpu.VMEM((ITERS - 1, nsec, 8, block), F32),
            pltpu.VMEM((ITERS - 1, 8, block), F32),
            pltpu.VMEM((2, half, block), BF16),
            pltpu.VMEM((pair, 8, block), F32),
            pltpu.VMEM((pair, 8, block), F32),
            pltpu.VMEM((8, block), F32),
            dma((4,)),
            dma((2, 2)),
            dma((2, 2)),
            dma,
            dma,
            dma((3, 2)),
            dma((3, 2)),
            dma((ITERS - 1, 3)),
            dma((ITERS - 1, 3)),
            dma((ITERS - 1, nsec)),
            dma((ITERS - 1, nsec)),
            dma((2,)),
            dma((2,)),
            dma((pair,)),
            dma((pair,)),
            dma((pair,)),
            dma((pair,)),
        ],
        compiler_params=pltpu.CompilerParams(
            collective_id=0, has_side_effects=True, vmem_limit_bytes=40 * 2**20
        ),
    )(
        sector_sizes,
        corners.reshape(2, half, block),
        edges.reshape(2, block, width),
        projectors.reshape(2, half, width),
    )
    return new.reshape(corners.shape), logs[None]


def solution(mesh):
    in_specs = (
        P(("grp", "col"), None, "sec", "rep", None),
        P(("grp", "col"), None, "sec", None, None),
        P(("grp", "col"), None, "sec", "rep", None),
        P(),
    )
    out_specs = (P(("grp", "col"), None, "sec", "rep", None), P(("grp", "col"), None, None))
    return jax.shard_map(
        functools.partial(on_device, mesh.shape["col"], mesh.shape["sec"]),
        mesh=mesh, in_specs=in_specs, out_specs=out_specs, check_vma=False,
    )
```

```python
import functools

import jax
import jax.numpy as jnp
from jax import lax
from jax.experimental import pallas as pl
from jax.experimental.pallas import tpu as pltpu
from jax.sharding import PartitionSpec as P

K_NEG = 16
K_ZERO = 17
ITERS = 4
MESH = pl.DeviceIdType.MESH
F32 = jnp.float32
BF16 = jnp.bfloat16


def rolled(x, axis):
    half = x.shape[axis] // 2
    lo = lax.slice_in_dim(x, 0, half, axis=axis)
    hi = lax.slice_in_dim(x, half, 2 * half, axis=axis)
    return jnp.concatenate([hi, lo], axis=axis)


def kernel(
    ncol, nsec, block, states, narrow,
    sizes_in, corners_in, edges, projectors,
    out, logs,
    sizes, corners, own, stage, packed, halo, proj, projt, first, cur, sent, scale, tiles, fin, last, all_last, last_tile,
    load_sem, halo_send, halo_recv, proj_send, proj_recv, first_send, first_recv,
    cur_send, cur_recv, scale_send, scale_recv, fin_send, fin_recv, next_send, next_recv, log_send, log_recv,
):
    half = block // 2
    rise = K_NEG + K_ZERO
    wide = K_NEG * block // 2
    c, t, r = lax.axis_index("col"), lax.axis_index("sec"), lax.axis_index("rep")
    other = 1 - r
    right = lax.rem(c + 1, ncol)
    pair = 2 * nsec
    me = t * 2 + r

    load_own = pltpu.make_async_copy(
        edges.at[r, :, K_NEG * block : rise * block], own, load_sem.at[0]
    )
    load_proj = pltpu.make_async_copy(projectors.at[r], proj.at[r], load_sem.at[1])
    loads = []
    if narrow:
        loads = [
            pltpu.make_async_copy(edges.at[r, :, rise * block :], stage.at[0], load_sem.at[2]),
            pltpu.make_async_copy(edges.at[r, :, : K_NEG * block], stage.at[1], load_sem.at[3]),
        ]
    load_sizes = pltpu.make_async_copy(sizes_in, sizes, load_sem.at[4])
    load_corners = pltpu.make_async_copy(corners_in, corners, load_sem.at[5])
    for copy in [load_sizes, load_corners] + loads + [load_proj, load_own]:
        copy.start()

    barrier = pltpu.get_barrier_semaphore()
    everyone = ncol * pair
    spot = c * pair + me

    @pl.loop(1, everyone)
    def _(step):
        to = lax.rem(spot + step, everyone)
        pl.semaphore_signal(
            barrier, inc=1,
            device_id={"col": to // pair, "sec": lax.rem(to, pair) // 2, "rep": lax.rem(to, 2)},
            device_id_type=MESH,
        )

    load_sizes.wait()
    live = sizes[t]
    count = jnp.float32(0.0)
    for s in range(nsec):
        size = sizes[s].astype(F32)
        count = count + size * size
    rows = lax.broadcasted_iota(jnp.int32, (block, block), 0)
    lanes = lax.broadcasted_iota(jnp.int32, (block, block), 1)
    keep = (rows < live) & (lanes < live)
    half_rows = lax.broadcasted_iota(jnp.int32, (half, block), 0) + r * half
    half_lanes = lax.broadcasted_iota(jnp.int32, (half, block), 1)
    half_keep = (half_rows < live) & (half_lanes < live)
    load_corners.wait()
    for which in range(2):
        value = corners[which].astype(F32)
        first[which] = jnp.where(half_keep, value, 0.0).astype(BF16)

    @pl.when(t == 0)
    def _():
        cur[:, 0] = jnp.zeros((ITERS, 2, half, block), BF16)
        halo[0] = jnp.zeros((2, block, wide), BF16)

    @pl.when(t == nsec - 1)
    def _():
        cur[:, 2] = jnp.zeros((ITERS, 2, half, block), BF16)
        halo[1] = jnp.zeros((2, block, wide), BF16)

    for side in range(len(loads)):
        loads[side].wait()
        for j in range(K_NEG // 2):
            low = stage[side, :, j * block : (j + 1) * block]
            high = stage[side, :, wide + j * block : wide + (j + 1) * block]
            by_row = jnp.concatenate([low[:half], high[:half]], axis=0)
            by_lane = jnp.concatenate([low[:, :half], high[:, :half]], axis=1)
            mixed = jnp.where(live > half, by_lane.astype(F32), by_row.astype(F32))
            packed[side, :, j * block : (j + 1) * block] = mixed.astype(BF16)

    pl.semaphore_wait(barrier, everyone - 1)

    has_low, has_high = t > 0, t < nsec - 1

    def guarded(dt, action):
        if dt == 0:
            action()
        else:
            pl.when(has_high if dt > 0 else has_low)(action)

    def halo_copy(side, part):
        if narrow:
            src = packed.at[side]
        else:
            start = (rise * block if side == 0 else 0) + part * wide
            src = edges.at[r, :, start : start + wide]
        return pltpu.make_async_remote_copy(
            src_ref=src, dst_ref=halo.at[side, part],
            send_sem=halo_send.at[side, part], recv_sem=halo_recv.at[side, part],
            device_id={"sec": t + 1 - 2 * side}, device_id_type=MESH,
        )

    parts = 1 if narrow else 2
    for side in range(2):

        def go(side=side):
            for part in range(parts):
                halo_copy(side, part).start()

        guarded(1 - 2 * side, go)

    send_proj = pltpu.make_async_remote_copy(
        src_ref=projectors.at[other], dst_ref=proj.at[r],
        send_sem=proj_send, recv_sem=proj_recv,
        device_id={"rep": other}, device_id_type=MESH,
    )
    send_proj.start()

    def first_copy(dt, which):
        side = r if which == 0 else other
        return pltpu.make_async_remote_copy(
            src_ref=first.at[side], dst_ref=cur.at[0, 1 - dt, r],
            send_sem=first_send.at[dt + 1, which], recv_sem=first_recv.at[1 - dt, which],
            device_id={"sec": t + dt, "rep": side}, device_id_type=MESH,
        )

    firsts = [(0, 1), (1, 0), (1, 1), (-1, 0), (-1, 1)]
    for dt, which in firsts:
        guarded(dt, lambda dt=dt, which=which: first_copy(dt, which).start())
    cur[0, 1, r] = first[r]

    load_proj.wait()
    send_proj.wait_recv()
    for k in range(states):
        piece = proj[:, :, k * block : (k + 1) * block].reshape(block, block)
        projt[:, k * block : (k + 1) * block] = piece.T
    load_own.wait()

    def part_of(corner, edge, start):
        number = edge.shape[1] // block
        absorbed = jnp.dot(corner, edge, preferred_element_type=F32).astype(BF16)
        stacked = jnp.concatenate(
            [absorbed[:, k * block : (k + 1) * block] for k in range(number)], axis=0
        )
        left = projt[:, start * block : (start + number) * block]
        return jnp.dot(left, stacked, preferred_element_type=F32)

    def halo_ready(side):
        def wait():
            for part in range(parts):
                halo_copy(side, part).wait_recv()

        guarded(2 * side - 1, wait)
        if narrow:
            source = jnp.clip(t - 1 + 2 * side, 0, nsec - 1)
            wide_rows = sizes[source] > half

            for j in range(K_NEG // 2):
                piece = halo[side, 0, :, j * block : (j + 1) * block]
                by_row, by_lane = rolled(piece, 0), rolled(piece, 1)
                mixed = jnp.where(wide_rows, by_lane.astype(F32), by_row.astype(F32))
                halo[side, 1, :, j * block : (j + 1) * block] = mixed.astype(BF16)

    def cur_copy(move, dt):
        return pltpu.make_async_remote_copy(
            src_ref=sent.at[move], dst_ref=cur.at[move + 1, 1 - dt],
            send_sem=cur_send.at[move, dt + 1], recv_sem=cur_recv.at[move, 1 - dt],
            device_id={"col": right, "sec": t + dt}, device_id_type=MESH,
        )

    def scale_copy(move, step):
        to = lax.rem(t + step, nsec)
        return pltpu.make_async_remote_copy(
            src_ref=tiles.at[move], dst_ref=scale.at[move, t],
            send_sem=scale_send.at[move, step], recv_sem=scale_recv.at[move, t],
            device_id={"col": right, "sec": to}, device_id_type=MESH,
        )

    def fin_copy(piece):
        return pltpu.make_async_remote_copy(
            src_ref=sent.at[ITERS - 1, piece], dst_ref=fin.at[r],
            send_sem=fin_send.at[piece], recv_sem=fin_recv.at[r],
            device_id={"col": right, "rep": jnp.int32(piece)}, device_id_type=MESH,
        )

    def spread_copy(step, same):
        to = lax.rem(me + step, pair)
        where = {"sec": to // 2, "rep": lax.rem(to, 2)}
        if not same:
            where["col"] = right
        sems, got, dst = (log_send, log_recv, all_last) if same else (next_send, next_recv, last)
        return pltpu.make_async_remote_copy(
            src_ref=last_tile, dst_ref=dst.at[me],
            send_sem=sems.at[step], recv_sem=got.at[me],
            device_id=where, device_id_type=MESH,
        )

    def arrived(ref, sem):
        pltpu.make_async_copy(ref, ref, sem).wait()

    def corner_ready(move, j):
        def wait():
            if move == 0:
                for which in range(2):
                    if j == 1 and which == 0:
                        continue
                    spot_ = cur.at[0, j, r if which == 0 else other]
                    arrived(spot_, first_recv.at[j, which])
            else:
                arrived(cur.at[move, j], cur_recv.at[move - 1, j])

        guarded(j - 1, wait)
        return cur[move, j].reshape(block, block)

    sums = []
    for move in range(ITERS):
        total = part_of(corner_ready(move, 1), own[...], K_NEG)
        for side, j, start in ((0, 0, rise), (1, 2, 0)):
            corner = corner_ready(move, j)
            if move == 0:
                halo_ready(side)
            for part in range(2):
                total = total + part_of(corner, halo[side, part], start + part * K_NEG // 2)
        if move > 0:
            for s in range(nsec):
                arrived(scale.at[move - 1, s], scale_recv.at[move - 1, s])
            whole = jnp.sum(jnp.sum(scale[move - 1], axis=0), keepdims=True)
            total = total / jnp.sqrt(whole / count + 1e-06)
        masked = jnp.where(keep, total, 0.0)
        sent[move] = masked.astype(BF16).reshape(2, half, block)
        if move < ITERS - 1:
            for dt in (0, 1, -1):
                guarded(dt, lambda dt=dt, move=move: cur_copy(move, dt).start())
        else:
            for piece in range(2):
                fin_copy(piece).start()
        squares = jnp.sum((masked * masked).reshape(block // 8, 8, block), axis=0)
        sums.append(jnp.sum(squares, axis=0, keepdims=True))
        if move < ITERS - 1:
            tiles[move] = squares
            for step in range(nsec):
                scale_copy(move, step).start()

    last_tile[...] = jnp.concatenate(sums + [jnp.zeros((8 - ITERS, block), F32)], axis=0)
    for step in range(pair):
        spread_copy(step, False).start()
    for step in range(1, pair):
        spread_copy(step, True).start()
    all_last[me] = last_tile[...]

    for s in range(pair):
        arrived(last.at[s], next_recv.at[s])
    for side in range(2):
        arrived(fin.at[side], fin_recv.at[side])
        whole = last[side]
        for s in range(1, nsec):
            whole = whole + last[2 * s + side]
        whole = jnp.sum(whole[ITERS - 1 : ITERS, :], keepdims=True)
        out[side] = (fin[side].astype(F32) / jnp.sqrt(whole / count + 1e-06)).astype(BF16)

    for step in range(1, pair):
        source = lax.rem(me + step, pair)
        arrived(all_last.at[source], log_recv.at[source])
    diagonal = lax.broadcasted_iota(jnp.int32, (8, block), 0) == lax.broadcasted_iota(
        jnp.int32, (8, block), 1
    )
    for side in range(2):
        whole = all_last[side]
        for s in range(1, nsec):
            whole = whole + all_last[2 * s + side]
        value = jnp.log(jnp.sum(whole, axis=1, keepdims=True) / count + 1e-06)
        row = jnp.sum(jnp.where(diagonal, value, 0.0), axis=0, keepdims=True)
        logs[side : side + 1, :] = row[:, :ITERS]

    send_proj.wait_send()
    for dt, which in firsts:
        guarded(dt, lambda dt=dt, which=which: first_copy(dt, which).wait_send())
    for side in range(2):

        def gone(side=side):
            for part in range(parts):
                halo_copy(side, part).wait_send()

        guarded(1 - 2 * side, gone)
    for move in range(ITERS - 1):
        for dt in (1, -1, 0):
            guarded(dt, lambda dt=dt, move=move: cur_copy(move, dt).wait_send())
        for step in range(nsec):
            scale_copy(move, step).wait_send()
    for piece in range(2):
        fin_copy(piece).wait_send()
    for step in range(pair):
        spread_copy(step, False).wait_send()
    for step in range(1, pair):
        spread_copy(step, True).wait_send()


def on_device(ncol, nsec, corners, edges, projectors, sector_sizes):
    half, block = corners.shape[3:]
    width = edges.shape[4]
    states = width // block
    pair = 2 * nsec
    narrow = 48 * nsec - block - (nsec - 2) <= half
    wide = K_NEG * block // 2
    dma = pltpu.SemaphoreType.DMA
    vmem = pl.BlockSpec(memory_space=pltpu.VMEM)
    anywhere = pl.BlockSpec(memory_space=pl.ANY)
    parked = (2, block, 2 * wide) if narrow else (2, 16, block)
    packed = (2, block, wide) if narrow else (2, 16, block)
    new, logs = pl.pallas_call(
        functools.partial(kernel, ncol, nsec, block, states, narrow),
        out_shape=(
            jax.ShapeDtypeStruct((2, half, block), BF16),
            jax.ShapeDtypeStruct((2, ITERS), F32),
        ),
        in_specs=[anywhere] * 4,
        out_specs=(vmem, vmem),
        scratch_shapes=[
            pltpu.SMEM((nsec,), jnp.int32),
            pltpu.VMEM((2, half, block), BF16),
            pltpu.VMEM((block, K_ZERO * block), BF16),
            pltpu.VMEM(parked, BF16),
            pltpu.VMEM(packed, BF16),
            pltpu.VMEM((2, 2, block, wide), BF16),
            pltpu.VMEM((2, half, width), BF16),
            pltpu.VMEM((block, width), BF16),
            pltpu.VMEM((2, half, block), BF16),
            pltpu.VMEM((ITERS, 3, 2, half, block), BF16),
            pltpu.VMEM((ITERS, 2, half, block), BF16),
            pltpu.VMEM((ITERS - 1, nsec, 8, block), F32),
            pltpu.VMEM((ITERS - 1, 8, block), F32),
            pltpu.VMEM((2, half, block), BF16),
            pltpu.VMEM((pair, 8, block), F32),
            pltpu.VMEM((pair, 8, block), F32),
            pltpu.VMEM((8, block), F32),
            dma((6,)),
            dma((2, 2)),
            dma((2, 2)),
            dma,
            dma,
            dma((3, 2)),
            dma((3, 2)),
            dma((ITERS - 1, 3)),
            dma((ITERS - 1, 3)),
            dma((ITERS - 1, nsec)),
            dma((ITERS - 1, nsec)),
            dma((2,)),
            dma((2,)),
            dma((pair,)),
            dma((pair,)),
            dma((pair,)),
            dma((pair,)),
        ],
        compiler_params=pltpu.CompilerParams(
            collective_id=0, has_side_effects=True, vmem_limit_bytes=60 * 2**20
        ),
    )(
        sector_sizes,
        corners.reshape(2, half, block),
        edges.reshape(2, block, width),
        projectors.reshape(2, half, width),
    )
    return new.reshape(corners.shape), logs[None]


def solution(mesh):
    in_specs = (
        P(("grp", "col"), None, "sec", "rep", None),
        P(("grp", "col"), None, "sec", None, None),
        P(("grp", "col"), None, "sec", "rep", None),
        P(),
    )
    out_specs = (P(("grp", "col"), None, "sec", "rep", None), P(("grp", "col"), None, None))
    return jax.shard_map(
        functools.partial(on_device, mesh.shape["col"], mesh.shape["sec"]),
        mesh=mesh, in_specs=in_specs, out_specs=out_specs, check_vma=False,
    )
```

```python
import functools

import jax
import jax.numpy as jnp
from jax import lax
from jax.experimental import pallas as pl
from jax.experimental.pallas import tpu as pltpu
from jax.sharding import PartitionSpec as P

K_NEG = 16
K_ZERO = 17
ITERS = 4
MESH = pl.DeviceIdType.MESH
F32 = jnp.float32
BF16 = jnp.bfloat16


def rolled(x, axis):
    half = x.shape[axis] // 2
    lo = lax.slice_in_dim(x, 0, half, axis=axis)
    hi = lax.slice_in_dim(x, half, 2 * half, axis=axis)
    return jnp.concatenate([hi, lo], axis=axis)


def kernel(
    ncol, nsec, block, states, narrow,
    sizes_in, corners_in, edges, projectors,
    out, logs,
    sizes, corners, own, stage, packed, halo, proj, projt, first, cur, sent, scale, tiles, fin, last, all_last, last_tile,
    load_sem, halo_send, halo_recv, proj_send, proj_recv, first_send, first_recv,
    cur_send, cur_recv, scale_send, scale_recv, fin_send, fin_recv, next_send, next_recv, log_send, log_recv, word,
):
    half = block // 2
    rise = K_NEG + K_ZERO
    wide = K_NEG * block // 2
    piece_wide = wide // 2
    c, t, r = lax.axis_index("col"), lax.axis_index("sec"), lax.axis_index("rep")
    other = 1 - r
    right = lax.rem(c + 1, ncol)
    pair = 2 * nsec
    me = t * 2 + r

    load_own = pltpu.make_async_copy(
        edges.at[r, :, K_NEG * block : rise * block], own, load_sem.at[0]
    )
    load_proj = pltpu.make_async_copy(projectors.at[r], proj.at[r], load_sem.at[1])
    loads = []
    if narrow:
        loads = [
            pltpu.make_async_copy(edges.at[r, :, rise * block :], stage.at[0], load_sem.at[2]),
            pltpu.make_async_copy(edges.at[r, :, : K_NEG * block], stage.at[1], load_sem.at[3]),
        ]
    load_sizes = pltpu.make_async_copy(sizes_in, sizes, load_sem.at[4])
    load_corners = pltpu.make_async_copy(corners_in, corners, load_sem.at[5])
    for copy in [load_sizes, load_corners] + loads + [load_proj, load_own]:
        copy.start()

    has_low, has_high = t > 0, t < nsec - 1

    def guarded(dt, action):
        if dt == 0:
            action()
        else:
            pl.when(has_high if dt > 0 else has_low)(action)

    barrier = pltpu.get_barrier_semaphore()

    def greet(where):
        pl.semaphore_signal(barrier, inc=1, device_id=where, device_id_type=MESH)

    columns = [right] if ncol == 2 else [right, lax.rem(c + ncol - 1, ncol)]
    greet({"rep": other})
    for column in columns:
        greet({"col": column})
        greet({"col": column, "rep": other})
    for dt in (1, -1):

        def greet_sector(dt=dt):
            greet({"sec": t + dt})
            greet({"sec": t + dt, "rep": other})

        guarded(dt, greet_sector)

    load_sizes.wait()
    live = sizes[t]
    count = jnp.float32(0.0)
    for s in range(nsec):
        size = sizes[s].astype(F32)
        count = count + size * size
    rows = lax.broadcasted_iota(jnp.int32, (block, block), 0)
    lanes = lax.broadcasted_iota(jnp.int32, (block, block), 1)
    keep = (rows < live) & (lanes < live)
    half_rows = lax.broadcasted_iota(jnp.int32, (half, block), 0) + r * half
    half_lanes = lax.broadcasted_iota(jnp.int32, (half, block), 1)
    half_keep = (half_rows < live) & (half_lanes < live)
    load_corners.wait()
    for which in range(2):
        value = corners[which].astype(F32)
        first[which] = jnp.where(half_keep, value, 0.0).astype(BF16)

    @pl.when(t == 0)
    def _():
        cur[:, 0] = jnp.zeros((ITERS, 2, half, block), BF16)
        halo[0] = jnp.zeros((block, 2 * wide), BF16)

    @pl.when(t == nsec - 1)
    def _():
        cur[:, 2] = jnp.zeros((ITERS, 2, half, block), BF16)
        halo[1] = jnp.zeros((block, 2 * wide), BF16)

    for side in range(len(loads)):
        loads[side].wait()
        for j in range(K_NEG // 2):
            low = stage[side, :, j * block : (j + 1) * block]
            high = stage[side, :, wide + j * block : wide + (j + 1) * block]
            by_row = jnp.concatenate([low[:half], high[:half]], axis=0)
            by_lane = jnp.concatenate([low[:, :half], high[:, :half]], axis=1)
            mixed = jnp.where(live > half, by_lane.astype(F32), by_row.astype(F32))
            place = slice(j % 4 * block, (j % 4 + 1) * block)
            packed[side, j // 4, :, place] = mixed.astype(BF16)

    lower = (t + nsec - 2) // (nsec - 1)
    upper = (2 * nsec - 3 - t) // (nsec - 1)
    pl.semaphore_wait(barrier, 1 + 2 * len(columns) + 2 * lower + 2 * upper)

    def pass_on(dt):
        pl.semaphore_signal(
            word.at[(dt + 1) // 2], inc=1, device_id={"sec": t + dt}, device_id_type=MESH
        )

    pl.when(t == 0)(lambda: pass_on(1))
    pl.when(t == nsec - 1)(lambda: pass_on(-1))

    def halo_copy(side, chunk, part):
        if narrow:
            src = packed.at[side, chunk]
        else:
            start = (rise * block if side == 0 else 0) + part * wide + chunk * piece_wide
            src = edges.at[r, :, start : start + piece_wide]
        return pltpu.make_async_remote_copy(
            src_ref=src, dst_ref=halo.at[side, :, part * wide + chunk * piece_wide : part * wide + (chunk + 1) * piece_wide],
            send_sem=halo_send.at[side, chunk, part], recv_sem=halo_recv.at[side, chunk, part],
            device_id={"sec": t + 1 - 2 * side}, device_id_type=MESH,
        )

    parts = 1 if narrow else 2
    for chunk in range(2):
        for side in range(2):

            def go(side=side, chunk=chunk):
                for part in range(parts):
                    halo_copy(side, chunk, part).start()

            guarded(1 - 2 * side, go)

    send_proj = pltpu.make_async_remote_copy(
        src_ref=projectors.at[other], dst_ref=proj.at[r],
        send_sem=proj_send, recv_sem=proj_recv,
        device_id={"rep": other}, device_id_type=MESH,
    )
    send_proj.start()

    def first_copy(dt, which):
        side = r if which == 0 else other
        return pltpu.make_async_remote_copy(
            src_ref=first.at[side], dst_ref=cur.at[0, 1 - dt, r],
            send_sem=first_send.at[dt + 1, which], recv_sem=first_recv.at[1 - dt, which],
            device_id={"sec": t + dt, "rep": side}, device_id_type=MESH,
        )

    firsts = [(0, 1), (1, 0), (1, 1), (-1, 0), (-1, 1)]
    for dt, which in firsts:
        guarded(dt, lambda dt=dt, which=which: first_copy(dt, which).start())
    cur[0, 1, r] = first[r]

    load_proj.wait()
    send_proj.wait_recv()
    for k in range(states):
        piece = proj[:, :, k * block : (k + 1) * block].reshape(block, block)
        projt[:, k * block : (k + 1) * block] = piece.T
    load_own.wait()

    between = jnp.logical_and(has_low, has_high)
    for dt in (1, -1):
        guarded(-dt, lambda dt=dt: pl.semaphore_wait(word.at[(dt + 1) // 2], 1))
        pl.when(between)(lambda dt=dt: pass_on(dt))

    def part_of(corner, edge, start):
        number = edge.shape[1] // block
        absorbed = jnp.dot(corner, edge, preferred_element_type=F32).astype(BF16)
        stacked = jnp.concatenate(
            [absorbed[:, k * block : (k + 1) * block] for k in range(number)], axis=0
        )
        left = projt[:, start * block : (start + number) * block]
        return jnp.dot(left, stacked, preferred_element_type=F32)

    def halo_ready(side, chunk):
        def wait():
            for part in range(parts):
                halo_copy(side, chunk, part).wait_recv()

        guarded(2 * side - 1, wait)
        if narrow:
            source = jnp.clip(t - 1 + 2 * side, 0, nsec - 1)
            wide_rows = sizes[source] > half

            for j in range(K_NEG // 4 * chunk, K_NEG // 4 * (chunk + 1)):
                piece = halo[side, :, j * block : (j + 1) * block]
                by_row, by_lane = rolled(piece, 0), rolled(piece, 1)
                mixed = jnp.where(wide_rows, by_lane.astype(F32), by_row.astype(F32))
                halo[side, :, wide + j * block : wide + (j + 1) * block] = mixed.astype(BF16)

    def cur_copy(move, dt):
        return pltpu.make_async_remote_copy(
            src_ref=sent.at[move], dst_ref=cur.at[move + 1, 1 - dt],
            send_sem=cur_send.at[move, dt + 1], recv_sem=cur_recv.at[move, 1 - dt],
            device_id={"col": right, "sec": t + dt}, device_id_type=MESH,
        )

    def scale_copy(move, step):
        to = lax.rem(t + step, nsec)
        return pltpu.make_async_remote_copy(
            src_ref=tiles.at[move], dst_ref=scale.at[move, t],
            send_sem=scale_send.at[move, step], recv_sem=scale_recv.at[move, t],
            device_id={"col": right, "sec": to}, device_id_type=MESH,
        )

    def fin_copy(piece):
        return pltpu.make_async_remote_copy(
            src_ref=sent.at[ITERS - 1, piece], dst_ref=fin.at[r],
            send_sem=fin_send.at[piece], recv_sem=fin_recv.at[r],
            device_id={"col": right, "rep": jnp.int32(piece)}, device_id_type=MESH,
        )

    def spread_copy(step, same):
        to = lax.rem(me + step, pair)
        where = {"sec": to // 2, "rep": lax.rem(to, 2)}
        if not same:
            where["col"] = right
        sems, got, dst = (log_send, log_recv, all_last) if same else (next_send, next_recv, last)
        return pltpu.make_async_remote_copy(
            src_ref=last_tile, dst_ref=dst.at[me],
            send_sem=sems.at[step], recv_sem=got.at[me],
            device_id=where, device_id_type=MESH,
        )

    def arrived(ref, sem):
        pltpu.make_async_copy(ref, ref, sem).wait()

    def corner_ready(move, j):
        def wait():
            if move == 0:
                for which in range(2):
                    if j == 1 and which == 0:
                        continue
                    spot_ = cur.at[0, j, r if which == 0 else other]
                    arrived(spot_, first_recv.at[j, which])
            else:
                arrived(cur.at[move, j], cur_recv.at[move - 1, j])

        guarded(j - 1, wait)
        return cur[move, j].reshape(block, block)

    sums = []
    for move in range(ITERS):
        total = part_of(corner_ready(move, 1), own[...], K_NEG)
        for side, j, start in ((0, 0, rise), (1, 2, 0)):
            corner = corner_ready(move, j)
            if move == 0:
                for chunk in range(2):
                    halo_ready(side, chunk)
            total = total + part_of(corner, halo[side], start)
        if move > 0:
            for s in range(nsec):
                arrived(scale.at[move - 1, s], scale_recv.at[move - 1, s])
            whole = jnp.sum(jnp.sum(scale[move - 1], axis=0), keepdims=True)
            total = total / jnp.sqrt(whole / count + 1e-06)
        masked = jnp.where(keep, total, 0.0)
        if move < ITERS - 1:
            sent[move] = masked.astype(BF16).reshape(2, half, block)
            for dt in (0, 1, -1):
                guarded(dt, lambda dt=dt, move=move: cur_copy(move, dt).start())
        squares = jnp.sum((masked * masked).reshape(block // 8, 8, block), axis=0)
        sums.append(jnp.sum(squares, axis=0, keepdims=True))
        if move < ITERS - 1:
            tiles[move] = squares
            for step in range(nsec):
                scale_copy(move, step).start()

    last_tile[...] = jnp.concatenate(sums + [jnp.zeros((8 - ITERS, block), F32)], axis=0)
    for step in range(pair - 1, -1, -1):
        spread_copy(step, False).start()
    sent[ITERS - 1] = masked.astype(BF16).reshape(2, half, block)
    for piece in range(2):
        fin_copy(piece).start()
    for step in range(1, pair):
        spread_copy(step, True).start()
    all_last[me] = last_tile[...]

    for s in range(pair):
        arrived(last.at[s], next_recv.at[s])
    for side in range(2):
        arrived(fin.at[side], fin_recv.at[side])
        whole = last[side]
        for s in range(1, nsec):
            whole = whole + last[2 * s + side]
        whole = jnp.sum(whole[ITERS - 1 : ITERS, :], keepdims=True)
        out[side] = (fin[side].astype(F32) / jnp.sqrt(whole / count + 1e-06)).astype(BF16)

    for step in range(1, pair):
        source = lax.rem(me + step, pair)
        arrived(all_last.at[source], log_recv.at[source])
    diagonal = lax.broadcasted_iota(jnp.int32, (8, block), 0) == lax.broadcasted_iota(
        jnp.int32, (8, block), 1
    )
    for side in range(2):
        whole = all_last[side]
        for s in range(1, nsec):
            whole = whole + all_last[2 * s + side]
        value = jnp.log(jnp.sum(whole, axis=1, keepdims=True) / count + 1e-06)
        row = jnp.sum(jnp.where(diagonal, value, 0.0), axis=0, keepdims=True)
        logs[side : side + 1, :] = row[:, :ITERS]

    send_proj.wait_send()
    for dt, which in firsts:
        guarded(dt, lambda dt=dt, which=which: first_copy(dt, which).wait_send())
    for side in range(2):

        def gone(side=side):
            for chunk in range(2):
                for part in range(parts):
                    halo_copy(side, chunk, part).wait_send()

        guarded(1 - 2 * side, gone)
    for move in range(ITERS - 1):
        for dt in (1, -1, 0):
            guarded(dt, lambda dt=dt, move=move: cur_copy(move, dt).wait_send())
        for step in range(nsec):
            scale_copy(move, step).wait_send()
    for piece in range(2):
        fin_copy(piece).wait_send()
    for step in range(pair):
        spread_copy(step, False).wait_send()
    for step in range(1, pair):
        spread_copy(step, True).wait_send()


def on_device(ncol, nsec, corners, edges, projectors, sector_sizes):
    half, block = corners.shape[3:]
    width = edges.shape[4]
    states = width // block
    pair = 2 * nsec
    narrow = 48 * nsec - block - (nsec - 2) <= half
    wide = K_NEG * block // 2
    dma = pltpu.SemaphoreType.DMA
    vmem = pl.BlockSpec(memory_space=pltpu.VMEM)
    anywhere = pl.BlockSpec(memory_space=pl.ANY)
    parked = (2, block, 2 * wide) if narrow else (2, 16, block)
    packed = (2, 2, block, wide // 2) if narrow else (2, 2, 16, block)
    new, logs = pl.pallas_call(
        functools.partial(kernel, ncol, nsec, block, states, narrow),
        out_shape=(
            jax.ShapeDtypeStruct((2, half, block), BF16),
            jax.ShapeDtypeStruct((2, ITERS), F32),
        ),
        in_specs=[anywhere] * 4,
        out_specs=(vmem, vmem),
        scratch_shapes=[
            pltpu.SMEM((nsec,), jnp.int32),
            pltpu.VMEM((2, half, block), BF16),
            pltpu.VMEM((block, K_ZERO * block), BF16),
            pltpu.VMEM(parked, BF16),
            pltpu.VMEM(packed, BF16),
            pltpu.VMEM((2, block, 2 * wide), BF16),
            pltpu.VMEM((2, half, width), BF16),
            pltpu.VMEM((block, width), BF16),
            pltpu.VMEM((2, half, block), BF16),
            pltpu.VMEM((ITERS, 3, 2, half, block), BF16),
            pltpu.VMEM((ITERS, 2, half, block), BF16),
            pltpu.VMEM((ITERS - 1, nsec, 8, block), F32),
            pltpu.VMEM((ITERS - 1, 8, block), F32),
            pltpu.VMEM((2, half, block), BF16),
            pltpu.VMEM((pair, 8, block), F32),
            pltpu.VMEM((pair, 8, block), F32),
            pltpu.VMEM((8, block), F32),
            dma((6,)),
            dma((2, 2, 2)),
            dma((2, 2, 2)),
            dma,
            dma,
            dma((3, 2)),
            dma((3, 2)),
            dma((ITERS - 1, 3)),
            dma((ITERS - 1, 3)),
            dma((ITERS - 1, nsec)),
            dma((ITERS - 1, nsec)),
            dma((2,)),
            dma((2,)),
            dma((pair,)),
            dma((pair,)),
            dma((pair,)),
            dma((pair,)),
            pltpu.SemaphoreType.REGULAR((2,)),
        ],
        compiler_params=pltpu.CompilerParams(
            collective_id=0, has_side_effects=True, vmem_limit_bytes=60 * 2**20
        ),
    )(
        sector_sizes,
        corners.reshape(2, half, block),
        edges.reshape(2, block, width),
        projectors.reshape(2, half, width),
    )
    return new.reshape(corners.shape), logs[None]


def solution(mesh):
    in_specs = (
        P(("grp", "col"), None, "sec", "rep", None),
        P(("grp", "col"), None, "sec", None, None),
        P(("grp", "col"), None, "sec", "rep", None),
        P(),
    )
    out_specs = (P(("grp", "col"), None, "sec", "rep", None), P(("grp", "col"), None, None))
    return jax.shard_map(
        functools.partial(on_device, mesh.shape["col"], mesh.shape["sec"]),
        mesh=mesh, in_specs=in_specs, out_specs=out_specs, check_vma=False,
    )
```

```python
import functools

import jax
import jax.numpy as jnp
from jax import lax
from jax.experimental import pallas as pl
from jax.experimental.pallas import tpu as pltpu
from jax.sharding import PartitionSpec as P

K_NEG = 16
K_ZERO = 17
ITERS = 4
MESH = pl.DeviceIdType.MESH
F32 = jnp.float32
BF16 = jnp.bfloat16


def rolled(x, axis):
    half = x.shape[axis] // 2
    lo = lax.slice_in_dim(x, 0, half, axis=axis)
    hi = lax.slice_in_dim(x, half, 2 * half, axis=axis)
    return jnp.concatenate([hi, lo], axis=axis)


def kernel(
    ncol, nsec, block, states, narrow,
    sizes_in, corners_in, edges, projectors,
    out, logs,
    sizes, corners, own, stage, packed, halo, proj, projt, first, cur, sent, scale, tiles, fin, last, all_last, last_tile,
    load_sem, halo_send, halo_recv, proj_send, proj_recv, first_send, first_recv,
    cur_send, cur_recv, scale_send, scale_recv, fin_send, fin_recv, next_send, next_recv, log_send, log_recv, word,
):
    half = block // 2
    rise = K_NEG + K_ZERO
    wide = K_NEG * block // 2
    piece_wide = wide // 2
    c, t, r = lax.axis_index("col"), lax.axis_index("sec"), lax.axis_index("rep")
    other = 1 - r
    right = lax.rem(c + 1, ncol)
    pair = 2 * nsec
    me = t * 2 + r

    load_own = pltpu.make_async_copy(
        edges.at[r, :, K_NEG * block : rise * block], own, load_sem.at[0]
    )
    load_proj = pltpu.make_async_copy(projectors.at[r], proj.at[r], load_sem.at[1])
    loads = []
    if narrow:
        loads = [
            pltpu.make_async_copy(edges.at[r, :, rise * block :], stage.at[0], load_sem.at[2]),
            pltpu.make_async_copy(edges.at[r, :, : K_NEG * block], stage.at[1], load_sem.at[3]),
        ]
    load_sizes = pltpu.make_async_copy(sizes_in, sizes, load_sem.at[4])
    load_corners = pltpu.make_async_copy(corners_in, corners, load_sem.at[5])
    for copy in [load_sizes, load_corners] + loads + [load_proj, load_own]:
        copy.start()

    has_low, has_high = t > 0, t < nsec - 1

    def guarded(dt, action):
        if dt == 0:
            action()
        else:
            pl.when(has_high if dt > 0 else has_low)(action)

    barrier = pltpu.get_barrier_semaphore()

    def greet(where):
        pl.semaphore_signal(barrier, inc=1, device_id=where, device_id_type=MESH)

    columns = [right] if ncol == 2 else [right, lax.rem(c + ncol - 1, ncol)]
    greet({"rep": other})
    for column in columns:
        greet({"col": column})
        greet({"col": column, "rep": other})
    for dt in (1, -1):

        def greet_sector(dt=dt):
            greet({"sec": t + dt})
            greet({"sec": t + dt, "rep": other})

        guarded(dt, greet_sector)

    load_sizes.wait()
    live = sizes[t]
    count = jnp.float32(0.0)
    for s in range(nsec):
        size = sizes[s].astype(F32)
        count = count + size * size
    rows = lax.broadcasted_iota(jnp.int32, (block, block), 0)
    lanes = lax.broadcasted_iota(jnp.int32, (block, block), 1)
    keep = (rows < live) & (lanes < live)
    half_rows = lax.broadcasted_iota(jnp.int32, (half, block), 0) + r * half
    half_lanes = lax.broadcasted_iota(jnp.int32, (half, block), 1)
    half_keep = (half_rows < live) & (half_lanes < live)
    load_corners.wait()
    for which in range(2):
        value = corners[which].astype(F32)
        first[which] = jnp.where(half_keep, value, 0.0).astype(BF16)

    @pl.when(t == 0)
    def _():
        cur[:, 0] = jnp.zeros((ITERS, 2, half, block), BF16)
        halo[0] = jnp.zeros((block, 2 * wide), BF16)

    @pl.when(t == nsec - 1)
    def _():
        cur[:, 2] = jnp.zeros((ITERS, 2, half, block), BF16)
        halo[1] = jnp.zeros((block, 2 * wide), BF16)

    for side in range(len(loads)):
        loads[side].wait()
        for j in range(K_NEG // 2):
            low = stage[side, :, j * block : (j + 1) * block]
            high = stage[side, :, wide + j * block : wide + (j + 1) * block]
            by_row = jnp.concatenate([low[:half], high[:half]], axis=0)
            by_lane = jnp.concatenate([low[:, :half], high[:, :half]], axis=1)
            mixed = jnp.where(live > half, by_lane.astype(F32), by_row.astype(F32))
            place = slice(j % 4 * block, (j % 4 + 1) * block)
            packed[side, j // 4, :, place] = mixed.astype(BF16)

    lower = (t + nsec - 2) // (nsec - 1)
    upper = (2 * nsec - 3 - t) // (nsec - 1)
    pl.semaphore_wait(barrier, 1 + 2 * len(columns) + 2 * lower + 2 * upper)

    def pass_on(dt):
        pl.semaphore_signal(
            word.at[(dt + 1) // 2], inc=1, device_id={"sec": t + dt}, device_id_type=MESH
        )

    pl.when(t == 0)(lambda: pass_on(1))
    pl.when(t == nsec - 1)(lambda: pass_on(-1))

    def halo_copy(side, chunk, part):
        if narrow:
            src = packed.at[side, chunk]
        else:
            start = (rise * block if side == 0 else 0) + part * wide + chunk * piece_wide
            src = edges.at[r, :, start : start + piece_wide]
        return pltpu.make_async_remote_copy(
            src_ref=src, dst_ref=halo.at[side, :, part * wide + chunk * piece_wide : part * wide + (chunk + 1) * piece_wide],
            send_sem=halo_send.at[side, chunk, part], recv_sem=halo_recv.at[side, chunk, part],
            device_id={"sec": t + 1 - 2 * side}, device_id_type=MESH,
        )

    parts = 1 if narrow else 2
    for chunk in range(2):
        for side in range(2):

            def go(side=side, chunk=chunk):
                for part in range(parts):
                    halo_copy(side, chunk, part).start()

            guarded(1 - 2 * side, go)

    send_proj = pltpu.make_async_remote_copy(
        src_ref=projectors.at[other], dst_ref=proj.at[r],
        send_sem=proj_send, recv_sem=proj_recv,
        device_id={"rep": other}, device_id_type=MESH,
    )
    send_proj.start()

    def first_copy(dt, which):
        side = r if which == 0 else other
        return pltpu.make_async_remote_copy(
            src_ref=first.at[side], dst_ref=cur.at[0, 1 - dt, r],
            send_sem=first_send.at[dt + 1, which], recv_sem=first_recv.at[1 - dt, which],
            device_id={"sec": t + dt, "rep": side}, device_id_type=MESH,
        )

    firsts = [(0, 1), (1, 0), (1, 1), (-1, 0), (-1, 1)]
    for dt, which in firsts:
        guarded(dt, lambda dt=dt, which=which: first_copy(dt, which).start())
    cur[0, 1, r] = first[r]

    load_proj.wait()
    send_proj.wait_recv()
    for k in range(states):
        piece = proj[:, :, k * block : (k + 1) * block].reshape(block, block)
        place = k - rise if k >= rise else k + K_NEG
        projt[:, place * block : (place + 1) * block] = piece.T
    load_own.wait()

    between = jnp.logical_and(has_low, has_high)
    for dt in (1, -1):
        guarded(-dt, lambda dt=dt: pl.semaphore_wait(word.at[(dt + 1) // 2], 1))
        pl.when(between)(lambda dt=dt: pass_on(dt))

    def absorb(corner, edge):
        absorbed = jnp.dot(corner, edge, preferred_element_type=F32).astype(BF16)
        return [absorbed[:, k : k + block] for k in range(0, edge.shape[1], block)]

    def project(pieces, start):
        stacked = jnp.concatenate(pieces, axis=0)
        left = projt[:, start * block : (start + len(pieces)) * block]
        return jnp.dot(left, stacked, preferred_element_type=F32)

    def halo_ready(side, chunk):
        def wait():
            for part in range(parts):
                halo_copy(side, chunk, part).wait_recv()

        guarded(2 * side - 1, wait)
        if narrow:
            source = jnp.clip(t - 1 + 2 * side, 0, nsec - 1)
            wide_rows = sizes[source] > half

            for j in range(K_NEG // 4 * chunk, K_NEG // 4 * (chunk + 1)):
                piece = halo[side, :, j * block : (j + 1) * block]
                by_row, by_lane = rolled(piece, 0), rolled(piece, 1)
                mixed = jnp.where(wide_rows, by_lane.astype(F32), by_row.astype(F32))
                halo[side, :, wide + j * block : wide + (j + 1) * block] = mixed.astype(BF16)

    def cur_copy(move, dt):
        return pltpu.make_async_remote_copy(
            src_ref=sent.at[move], dst_ref=cur.at[move + 1, 1 - dt],
            send_sem=cur_send.at[move, dt + 1], recv_sem=cur_recv.at[move, 1 - dt],
            device_id={"col": right, "sec": t + dt}, device_id_type=MESH,
        )

    def scale_copy(move, step):
        to = lax.rem(t + step, nsec)
        return pltpu.make_async_remote_copy(
            src_ref=tiles.at[move], dst_ref=scale.at[move, t],
            send_sem=scale_send.at[move, step], recv_sem=scale_recv.at[move, t],
            device_id={"col": right, "sec": to}, device_id_type=MESH,
        )

    def fin_copy(piece):
        return pltpu.make_async_remote_copy(
            src_ref=sent.at[ITERS - 1, piece], dst_ref=fin.at[r],
            send_sem=fin_send.at[piece], recv_sem=fin_recv.at[r],
            device_id={"col": right, "rep": jnp.int32(piece)}, device_id_type=MESH,
        )

    def spread_copy(step, same):
        to = lax.rem(me + step, pair)
        where = {"sec": to // 2, "rep": lax.rem(to, 2)}
        if not same:
            where["col"] = right
        sems, got, dst = (log_send, log_recv, all_last) if same else (next_send, next_recv, last)
        return pltpu.make_async_remote_copy(
            src_ref=last_tile, dst_ref=dst.at[me],
            send_sem=sems.at[step], recv_sem=got.at[me],
            device_id=where, device_id_type=MESH,
        )

    def arrived(ref, sem):
        pltpu.make_async_copy(ref, ref, sem).wait()

    def corner_ready(move, j):
        def wait():
            if move == 0:
                for which in range(2):
                    if j == 1 and which == 0:
                        continue
                    spot_ = cur.at[0, j, r if which == 0 else other]
                    arrived(spot_, first_recv.at[j, which])
            else:
                arrived(cur.at[move, j], cur_recv.at[move - 1, j])

        guarded(j - 1, wait)
        return cur[move, j].reshape(block, block)

    sums = []
    for move in range(ITERS):
        total = project(absorb(corner_ready(move, 1), own[...]), 2 * K_NEG)
        around = []
        for side, j in ((0, 0), (1, 2)):
            corner = corner_ready(move, j)
            if move == 0:
                for chunk in range(2):
                    halo_ready(side, chunk)
            around = around + absorb(corner, halo[side])
        total = total + project(around, 0)
        if move > 0:
            for s in range(nsec):
                arrived(scale.at[move - 1, s], scale_recv.at[move - 1, s])
            whole = jnp.sum(jnp.sum(scale[move - 1], axis=0), keepdims=True)
            total = total / jnp.sqrt(whole / count + 1e-06)
        masked = jnp.where(keep, total, 0.0)
        if move < ITERS - 1:
            sent[move] = masked.astype(BF16).reshape(2, half, block)
            for dt in (0, 1, -1):
                guarded(dt, lambda dt=dt, move=move: cur_copy(move, dt).start())
        squares = jnp.sum((masked * masked).reshape(block // 8, 8, block), axis=0)
        sums.append(jnp.sum(squares, axis=0, keepdims=True))
        if move < ITERS - 1:
            tiles[move] = squares
            for step in range(nsec):
                scale_copy(move, step).start()

    last_tile[...] = jnp.concatenate(sums + [jnp.zeros((8 - ITERS, block), F32)], axis=0)
    for step in range(pair - 1, -1, -1):
        spread_copy(step, False).start()
    sent[ITERS - 1] = masked.astype(BF16).reshape(2, half, block)
    for piece in range(2):
        fin_copy(piece).start()
    for step in range(1, pair):
        spread_copy(step, True).start()
    all_last[me] = last_tile[...]

    for s in range(pair):
        arrived(last.at[s], next_recv.at[s])
    for side in range(2):
        arrived(fin.at[side], fin_recv.at[side])
        whole = last[side]
        for s in range(1, nsec):
            whole = whole + last[2 * s + side]
        whole = jnp.sum(whole[ITERS - 1 : ITERS, :], keepdims=True)
        out[side] = (fin[side].astype(F32) / jnp.sqrt(whole / count + 1e-06)).astype(BF16)

    for step in range(1, pair):
        source = lax.rem(me + step, pair)
        arrived(all_last.at[source], log_recv.at[source])
    diagonal = lax.broadcasted_iota(jnp.int32, (8, block), 0) == lax.broadcasted_iota(
        jnp.int32, (8, block), 1
    )
    for side in range(2):
        whole = all_last[side]
        for s in range(1, nsec):
            whole = whole + all_last[2 * s + side]
        value = jnp.log(jnp.sum(whole, axis=1, keepdims=True) / count + 1e-06)
        row = jnp.sum(jnp.where(diagonal, value, 0.0), axis=0, keepdims=True)
        logs[side : side + 1, :] = row[:, :ITERS]

    send_proj.wait_send()
    for dt, which in firsts:
        guarded(dt, lambda dt=dt, which=which: first_copy(dt, which).wait_send())
    for side in range(2):

        def gone(side=side):
            for chunk in range(2):
                for part in range(parts):
                    halo_copy(side, chunk, part).wait_send()

        guarded(1 - 2 * side, gone)
    for move in range(ITERS - 1):
        for dt in (1, -1, 0):
            guarded(dt, lambda dt=dt, move=move: cur_copy(move, dt).wait_send())
        for step in range(nsec):
            scale_copy(move, step).wait_send()
    for piece in range(2):
        fin_copy(piece).wait_send()
    for step in range(pair):
        spread_copy(step, False).wait_send()
    for step in range(1, pair):
        spread_copy(step, True).wait_send()


def on_device(ncol, nsec, corners, edges, projectors, sector_sizes):
    half, block = corners.shape[3:]
    width = edges.shape[4]
    states = width // block
    pair = 2 * nsec
    narrow = 48 * nsec - block - (nsec - 2) <= half
    wide = K_NEG * block // 2
    dma = pltpu.SemaphoreType.DMA
    vmem = pl.BlockSpec(memory_space=pltpu.VMEM)
    anywhere = pl.BlockSpec(memory_space=pl.ANY)
    parked = (2, block, 2 * wide) if narrow else (2, 16, block)
    packed = (2, 2, block, wide // 2) if narrow else (2, 2, 16, block)
    new, logs = pl.pallas_call(
        functools.partial(kernel, ncol, nsec, block, states, narrow),
        out_shape=(
            jax.ShapeDtypeStruct((2, half, block), BF16),
            jax.ShapeDtypeStruct((2, ITERS), F32),
        ),
        in_specs=[anywhere] * 4,
        out_specs=(vmem, vmem),
        scratch_shapes=[
            pltpu.SMEM((nsec,), jnp.int32),
            pltpu.VMEM((2, half, block), BF16),
            pltpu.VMEM((block, K_ZERO * block), BF16),
            pltpu.VMEM(parked, BF16),
            pltpu.VMEM(packed, BF16),
            pltpu.VMEM((2, block, 2 * wide), BF16),
            pltpu.VMEM((2, half, width), BF16),
            pltpu.VMEM((block, width), BF16),
            pltpu.VMEM((2, half, block), BF16),
            pltpu.VMEM((ITERS, 3, 2, half, block), BF16),
            pltpu.VMEM((ITERS, 2, half, block), BF16),
            pltpu.VMEM((ITERS - 1, nsec, 8, block), F32),
            pltpu.VMEM((ITERS - 1, 8, block), F32),
            pltpu.VMEM((2, half, block), BF16),
            pltpu.VMEM((pair, 8, block), F32),
            pltpu.VMEM((pair, 8, block), F32),
            pltpu.VMEM((8, block), F32),
            dma((6,)),
            dma((2, 2, 2)),
            dma((2, 2, 2)),
            dma,
            dma,
            dma((3, 2)),
            dma((3, 2)),
            dma((ITERS - 1, 3)),
            dma((ITERS - 1, 3)),
            dma((ITERS - 1, nsec)),
            dma((ITERS - 1, nsec)),
            dma((2,)),
            dma((2,)),
            dma((pair,)),
            dma((pair,)),
            dma((pair,)),
            dma((pair,)),
            pltpu.SemaphoreType.REGULAR((2,)),
        ],
        compiler_params=pltpu.CompilerParams(
            collective_id=0, has_side_effects=True, vmem_limit_bytes=60 * 2**20
        ),
    )(
        sector_sizes,
        corners.reshape(2, half, block),
        edges.reshape(2, block, width),
        projectors.reshape(2, half, width),
    )
    def write(new_ref, logs_ref, new_out, logs_out, sems):
        copies = [
            pltpu.make_async_copy(new_ref, new_out, sems.at[0]),
            pltpu.make_async_copy(logs_ref, logs_out, sems.at[1]),
        ]
        for copy in copies:
            copy.start()
        for copy in copies:
            copy.wait()

    new, logs = pl.pallas_call(
        write,
        out_shape=(
            jax.ShapeDtypeStruct((2, half, block), BF16),
            jax.ShapeDtypeStruct((2, ITERS), F32),
        ),
        in_specs=[anywhere, anywhere],
        out_specs=(anywhere, anywhere),
        scratch_shapes=[dma((2,))],
        compiler_params=pltpu.CompilerParams(vmem_limit_bytes=60 * 2**20),
    )(new, logs)
    return new.reshape(corners.shape), logs[None]


def solution(mesh):
    in_specs = (
        P(("grp", "col"), None, "sec", "rep", None),
        P(("grp", "col"), None, "sec", None, None),
        P(("grp", "col"), None, "sec", "rep", None),
        P(),
    )
    out_specs = (P(("grp", "col"), None, "sec", "rep", None), P(("grp", "col"), None, None))
    return jax.shard_map(
        functools.partial(on_device, mesh.shape["col"], mesh.shape["sec"]),
        mesh=mesh, in_specs=in_specs, out_specs=out_specs, check_vma=False,
    )
```
